32 devices in a mesh: groups: 2 (over y), gx: 4 (over z), gy: 2 (over x), gz: 2 (over core).
Axes of the slice: x: 2, y: 2, z: 4, core: 2. Of those that a mesh axis runs over, the one named last changes fastest.
Arguments:
- coarse_state: float32 [8, 128, 32, 256], P(None, ('groups', 'gx'), 'gy', 'gz'), parts along dimension 1, may hold values from -6 to 6
- coarse_previous: float32 [8, 128, 32, 256], P(None, ('groups', 'gx'), 'gy', 'gz'), parts along dimension 1, may hold values from -6 to 6
- coarse_coefficient: float32 [2, 64, 32, 256], P(None, 'gx', 'gy', 'gz'), may hold values from 0.5 to 4
- fine_state: float32 [8, 128, 32, 256], P(None, ('groups', 'gx'), 'gy', 'gz'), parts along dimension 1, may hold values from -6 to 6
- fine_previous: float32 [8, 128, 32, 256], P(None, ('groups', 'gx'), 'gy', 'gz'), parts along dimension 1, may hold values from -6 to 6
- fine_coefficient: float32 [2, 64, 32, 256], P(None, 'gx', 'gy', 'gz'), may hold values from 0.5 to 4
- fine_parent: int32 [4, 2, 2, 2], P('gx', 'gy', 'gz'), may hold values from 0 to 3, as said below
- patch_dest: int32 [4, 2, 2, 2], P('gx', 'gy', 'gz'), may hold values from -1 to 3, as said below
Outputs:
- coarse_slope: float32 [8, 128, 32, 256], P(None, ('groups', 'gx'), 'gy', 'gz'), parts along dimension 1
- fine_slope: float32 [8, 128, 32, 256], P(None, ('groups', 'gx'), 'gy', 'gz'), parts along dimension 1
The draws below stay inside these ranges and needn't reach their ends.
There are 2 independent parts, one for each index of `groups`. The reference program is written for one: setup_inputs(seed, part) draws one part's arguments, and reference() takes and returns one part's arrays. A program takes and returns all parts, laid end to end along the dimension named above; an argument that names none is the same for every part. Nothing has to cross between parts.
Inputs may be any that keep to these rules, and one draw needn't show every extreme that they name: fine_parent[i, j, k] = (g, c): the fine box at (i, j, k) refines candidate patch c of brick (g, j, k); no two fine boxes refine the same patch; c is 0 or 1. patch_dest[g, j, k, c] = i exactly when fine_parent[i, j, k] = (g, c), else -1.
All inputs are finite; a program needn't handle non-finite values.
Results may differ from the reference program's by a relative error of at most 0.0003.
Values sent between devices are 32-bit elements; how exact they have to be, the bound alone decides.
A program may use at most 64 MiB of HBM per device.

```python
import math
import jax
import jax.numpy as jnp
from jax import lax

CX = 16
CY = 16
CZ = 128
PX = 8
PY = 8
PZ = 64
NX = 64
NY = 32
NZ = 256
N_GX = 4
N_GY = 2
N_GZ = 2


def layout(key):
    line_count = N_GY * N_GZ
    half_count = N_GX // 2
    first_key, second_key, third_key = jax.random.split(key, 3)
    run_start = jax.random.randint(first_key, (line_count,), 0, half_count + 1)
    marked = jax.random.randint(third_key, (), 0, line_count)
    run_start = run_start.at[marked].set(half_count)
    run_start = run_start.at[(marked + 1) % line_count].set(0)
    placement = jax.vmap(lambda subkey: jax.random.permutation(subkey, N_GX))(jax.random.split(second_key, line_count)).astype(jnp.int32)
    return (run_start.astype(jnp.int32), placement)


def draw_fine_parent(key, part):
    run_start, placement = layout(key)
    owner_slab = run_start[:, None] + placement // 2
    candidate = placement % 2
    stacked = jnp.stack([owner_slab, candidate], axis=-1)
    return stacked.transpose(1, 0, 2).reshape(N_GX, N_GY, N_GZ, 2).astype(jnp.int32)


def draw_patch_dest(key, part):
    run_start, placement = layout(key)
    half_count = N_GX // 2
    inverse = jnp.argsort(placement, axis=1).astype(jnp.int32)
    owner_slabs = jnp.arange(N_GX, dtype=jnp.int32)
    offset_rows = owner_slabs[None, :] - run_start[:, None]
    inside = (offset_rows >= 0) & (offset_rows < half_count)
    slot_index = 2 * jnp.clip(offset_rows, 0, half_count - 1)
    result = []
    for candidate in range(2):
        picked = jnp.take_along_axis(inverse, slot_index + candidate, axis=1)
        result.append(jnp.where(inside, picked, -1))
    stacked = jnp.stack(result, axis=-1)
    return stacked.transpose(1, 0, 2).reshape(N_GX, N_GY, N_GZ, 2).astype(jnp.int32)


def steps_of(rng, shape, cuts, smallest, top_value):
    level = 1.0
    for axis_at, parts in cuts:
        draws = jax.random.uniform(jax.random.fold_in(jax.random.fold_in(rng, 6), axis_at), (parts,), jnp.float32, smallest / len(cuts), top_value / len(cuts))
        level = level * jnp.repeat(jnp.exp(draws), shape[axis_at] // parts).reshape((-1,) + (1,) * (len(shape) - 1 - axis_at))
    return level


def noise(rng, dims, deviation, bound, shards=(), held_as=jnp.bfloat16):
    array = deviation * jax.random.normal(rng, dims, jnp.float32)
    if shards:
        array = array * steps_of(rng, dims, shards, -0.22, 0.18)
    return jnp.clip(array, -bound, bound).astype(held_as)


def setup_inputs(seed: int = 0, part: int = 0) -> dict:
    seeds = jax.random.split(jax.random.key(seed), 9)
    part_keys = jax.random.split(jax.random.fold_in(seeds[8], part), 9)
    coarse_state = noise(part_keys[0], (8, NX, NY, NZ), 1.0, 6.0, ((1, 4), (2, 2), (3, 2)), jnp.float32)
    coarse_previous = noise(part_keys[1], (8, NX, NY, NZ), 1.0, 6.0, ((1, 4), (2, 2), (3, 2)), jnp.float32)
    coarse_coefficient = jnp.clip(jnp.exp(math.log(4.0) - 2.0794415 * jax.random.uniform(seeds[2], (2, NX, NY, NZ), jnp.float32) ** steps_of(seeds[2], (2, NX, NY, NZ), ((1, 4), (2, 2), (3, 2)), -0.2, 0.2)), 0.5, 4.0)
    fine_state = noise(part_keys[3], (8, NX, NY, NZ), 1.0, 6.0, ((1, 4), (2, 2), (3, 2)), jnp.float32)
    fine_previous = noise(part_keys[4], (8, NX, NY, NZ), 1.0, 6.0, ((1, 4), (2, 2), (3, 2)), jnp.float32)
    fine_coefficient = jnp.clip(jnp.exp(math.log(4.0) - 2.0794415 * jax.random.uniform(seeds[5], (2, NX, NY, NZ), jnp.float32) ** steps_of(seeds[5], (2, NX, NY, NZ), ((1, 4), (2, 2), (3, 2)), -0.2, 0.2)), 0.5, 4.0)
    fine_parent = draw_fine_parent(jax.random.fold_in(seeds[8], 71), part)
    patch_dest = draw_patch_dest(jax.random.fold_in(seeds[8], 71), part)
    return {"coarse_state": coarse_state, "coarse_previous": coarse_previous, "coarse_coefficient": coarse_coefficient, "fine_state": fine_state, "fine_previous": fine_previous, "fine_coefficient": fine_coefficient, "fine_parent": fine_parent, "patch_dest": patch_dest}


section_weight = 0.1


def starts(values):
    return tuple(jnp.asarray(value).astype(jnp.int32) for value in values)


def operands(state, previous, coefficient):
    section_state = state + section_weight * previous
    modulus = coefficient[0]
    buoyancy = coefficient[1]
    return jnp.stack([section_state[0], section_state[1], section_state[2], section_state[3],
                      modulus * section_state[4], buoyancy * section_state[5],
                      buoyancy * section_state[6], buoyancy * section_state[7]])


def select_fields(fields, direction):
    return jnp.stack([fields[0], fields[1 + direction], fields[4], fields[5 + direction]])


def derivative(extended, axis_number, spacing):
    interior = extended.shape[axis_number] - 4

    def offset(initial):
        return lax.slice_in_dim(extended, initial, initial + interior, axis=axis_number)

    return (offset(0) - 8.0 * offset(1) + 8.0 * offset(3) - offset(4)) / (12.0 * spacing)


def slopes(extended, coefficient, spacing):
    derived = [derivative(extended[direction], direction + 1, spacing) for direction in range(3)]
    modulus = coefficient[0]
    buoyancy = coefficient[1]
    pressure_rate = -modulus * (derived[0][1] + derived[1][1] + derived[2][1])
    adjoint_rate = -(derived[0][3] + derived[1][3] + derived[2][3])
    return jnp.stack([pressure_rate, -buoyancy * derived[0][0], -buoyancy * derived[1][0],
                      -buoyancy * derived[2][0], adjoint_rate, -derived[0][2],
                      -derived[1][2], -derived[2][2]])


def upsample(face):
    return jnp.repeat(jnp.repeat(face, 2, axis=1), 2, axis=2)


def ghost_layers(face, direction):
    layered = jnp.expand_dims(upsample(face), direction + 1)
    shape_list = list(layered.shape)
    shape_list[direction + 1] = 2
    return jnp.broadcast_to(layered, tuple(shape_list))


def fine_extended(operand, lower_faces, upper_faces):
    return [jnp.concatenate([ghost_layers(lower_faces[direction], direction),
                             select_fields(operand, direction),
                             ghost_layers(upper_faces[direction], direction)], axis=direction + 1)
            for direction in range(3)]


def coarse_extended(padded):
    return [select_fields(padded, 0)[:, :, 2:-2, 2:-2],
            select_fields(padded, 1)[:, 2:-2, :, 2:-2],
            select_fields(padded, 2)[:, 2:-2, 2:-2, :]]


def reference(coarse_state, coarse_previous, coarse_coefficient, fine_state, fine_previous,
              fine_coefficient, fine_parent, patch_dest):
    coarse_operand = operands(coarse_state, coarse_previous, coarse_coefficient)
    padded = jnp.pad(coarse_operand, ((0, 0), (2, 2), (2, 2), (2, 2)))
    coarse_slope = slopes(coarse_extended(padded), coarse_coefficient, 1.0)
    line_count = N_GY * N_GZ

    def fine_box(number):
        number = number.astype(jnp.int32)
        slab_index = number // line_count
        cross_index = (number // N_GZ) % N_GY
        depth_index = number % N_GZ
        corner = starts((0, slab_index * CX, cross_index * CY, depth_index * CZ))
        box_state = lax.dynamic_slice(fine_state, corner, (8, CX, CY, CZ))
        previous = lax.dynamic_slice(fine_previous, corner, (8, CX, CY, CZ))
        coefficient = lax.dynamic_slice(fine_coefficient, corner, (2, CX, CY, CZ))
        parent = fine_parent[slab_index, cross_index, depth_index].astype(jnp.int32)
        candidate = parent[1]
        anchor = [parent[0] * CX + candidate * PX + 2,
                  cross_index * CY + candidate * PY + 2,
                  depth_index * CZ + candidate * PZ + 2]
        lower_faces = [
            lax.dynamic_slice(padded, starts((0, anchor[0] - 1, anchor[1], anchor[2])), (8, 1, PY, PZ))[:, 0],
            lax.dynamic_slice(padded, starts((0, anchor[0], anchor[1] - 1, anchor[2])), (8, PX, 1, PZ))[:, :, 0],
            lax.dynamic_slice(padded, starts((0, anchor[0], anchor[1], anchor[2] - 1)), (8, PX, PY, 1))[:, :, :, 0]]
        upper_faces = [
            lax.dynamic_slice(padded, starts((0, anchor[0] + PX, anchor[1], anchor[2])), (8, 1, PY, PZ))[:, 0],
            lax.dynamic_slice(padded, starts((0, anchor[0], anchor[1] + PY, anchor[2])), (8, PX, 1, PZ))[:, :, 0],
            lax.dynamic_slice(padded, starts((0, anchor[0], anchor[1], anchor[2] + PZ)), (8, PX, PY, 1))[:, :, :, 0]]
        lower_faces = [select_fields(lower_faces[direction], direction) for direction in range(3)]
        upper_faces = [select_fields(upper_faces[direction], direction) for direction in range(3)]
        operand = operands(box_state, previous, coefficient)
        return slopes(fine_extended(operand, lower_faces, upper_faces), coefficient, 0.5)

    box_slopes = lax.map(fine_box, jnp.arange(N_GX * line_count, dtype=jnp.int32))
    box_slopes = box_slopes.reshape(N_GX, N_GY, N_GZ, 8, CX, CY, CZ)
    fine_slope = box_slopes.transpose(3, 0, 4, 1, 5, 2, 6).reshape(8, CX * N_GX, CY * N_GY, CZ * N_GZ)
    averaged = box_slopes.reshape(N_GX, N_GY, N_GZ, 8, PX, 2, PY, 2, PZ, 2).sum(axis=(5, 7, 9)) * 0.125
    blocks = coarse_slope.reshape(8, N_GX, CX, N_GY, CY, N_GZ, CZ)
    cross_rows = jnp.arange(N_GY, dtype=jnp.int32)[None, :, None]
    depth_rows = jnp.arange(N_GZ, dtype=jnp.int32)[None, None, :]
    for candidate in range(2):
        target = patch_dest[:, :, :, candidate].astype(jnp.int32)
        gathered = averaged[jnp.maximum(target, 0), cross_rows, depth_rows]
        gathered = gathered.transpose(3, 0, 4, 1, 5, 2, 6)
        window = (slice(None), slice(None), slice(candidate * PX, (candidate + 1) * PX), slice(None),
                  slice(candidate * PY, (candidate + 1) * PY), slice(None),
                  slice(candidate * PZ, (candidate + 1) * PZ))
        region = blocks[window]
        refined = (target >= 0)[None, :, None, :, None, :, None]
        blocks = blocks.at[window].set(jnp.where(refined, gathered, region))
    coarse_slope = blocks.reshape(8, CX * N_GX, CY * N_GY, CZ * N_GZ)
    return coarse_slope, fine_slope
```

```python
import functools

import jax
import jax.numpy as jnp
from jax import lax
from jax.experimental import pallas as pl
from jax.experimental.pallas import tpu as pltpu
from jax.sharding import PartitionSpec as P

section_weight = 0.1
MESH = pl.DeviceIdType.MESH
x_fields = (0, 1, 4, 5)
y_fields = (0, 2, 4, 6)
z_fields = (0, 3, 4, 7)


def split_dot(values, matrix):
    high = values.astype(jnp.bfloat16)
    low = (values - high.astype(jnp.float32)).astype(jnp.bfloat16)
    return jnp.dot(high, matrix, preferred_element_type=jnp.float32) + jnp.dot(
        low, matrix, preferred_element_type=jnp.float32
    )


def kernel(
    counts,
    parent_ref,
    dest_ref,
    cs_hbm,
    cp_hbm,
    cc_hbm,
    fs_hbm,
    fp_hbm,
    fc_hbm,
    co_hbm,
    fo_hbm,
    cs,
    cp,
    cc,
    fs,
    fp,
    fc,
    cop,
    fop,
    cez,
    fez,
    co,
    fo,
    ysend,
    yhalo,
    zsend,
    zhalo,
    rim_pair,
    rim_send,
    rim_recv,
    zup,
    xup,
    pairs,
    avg,
    in_sem,
    out_sem,
    hx_send,
    hx_recv,
    hy_send,
    hy_recv,
    hz_send,
    hz_recv,
    rim_ss,
    rim_rs,
    avg_ss,
    avg_rs,
):
    count_x, count_y, count_z = counts
    CX, CY, CZ = cs.shape[1:]
    PX, PY, PZ = CX // 2, CY // 2, CZ // 2
    me = lax.axis_index("gx")
    my = lax.axis_index("gy")
    mz = lax.axis_index("gz")
    loads = [
        pltpu.make_async_copy(source, target, in_sem.at[number])
        for number, (source, target) in enumerate(
            ((cs_hbm, cs), (cp_hbm, cp), (cc_hbm, cc), (fs_hbm, fs), (fp_hbm, fp), (fc_hbm, fc))
        )
    ]
    for load in loads:
        load.start()

    peers = [lax.rem(me + offset, count_x) for offset in range(count_x)]
    barrier = pltpu.get_barrier_semaphore()
    for offset in range(1, count_x):
        pl.semaphore_signal(barrier, inc=1, device_id={"gx": peers[offset]}, device_id_type=MESH)
    has = {
        ("gx", 0): me > 0,
        ("gx", 1): me < count_x - 1,
        ("gy", 0): my > 0,
        ("gy", 1): my < count_y - 1,
        ("gz", 0): mz > 0,
        ("gz", 1): mz < count_z - 1,
    }
    index = {"gx": me, "gy": my, "gz": mz}
    count = {"gx": count_x, "gy": count_y, "gz": count_z}

    def neighbour(axis, side):
        return {axis: lax.rem(index[axis] + (1 if side else count[axis] - 1), count[axis])}

    for axis in ("gy", "gz"):
        for side in range(2):

            @pl.when(has[axis, side])
            def _():
                pl.semaphore_signal(
                    barrier, inc=1, device_id=neighbour(axis, side), device_id_type=MESH
                )

    expected = count_x - 1
    for axis in ("gy", "gz"):
        for side in range(2):
            expected = expected + has[axis, side].astype(jnp.int32)

    lane = lax.broadcasted_iota(jnp.int32, (CY, CZ), 1)
    lane_half = lax.broadcasted_iota(jnp.int32, (PY, CZ), 1)
    inner = slice(8, 8 + CY)

    def operands(state, previous, coefficient, target):
        def step(x, carry):
            modulus = coefficient[0, x]
            buoyancy = coefficient[1, x]
            for field in range(8):
                value = state[field, x] + section_weight * previous[field, x]
                if field == 4:
                    value = modulus * value
                if field > 4:
                    value = buoyancy * value
                target[field, x + 2, inner, :] = value
            return carry

        lax.fori_loop(0, CX, step, 0)

    def slopes(op, ez, coefficient, out, scale):
        def step(x, carry):
            modulus = coefficient[0, x]
            buoyancy = coefficient[1, x]

            def dx(field):
                return scale * (
                    (op[field, x, inner, :] - op[field, x + 4, inner, :])
                    - 8.0 * (op[field, x + 1, inner, :] - op[field, x + 3, inner, :])
                )

            def dy(field):
                return scale * (
                    (op[field, x + 2, 6 : 6 + CY, :] - op[field, x + 2, 10 : 10 + CY, :])
                    - 8.0 * (op[field, x + 2, 7 : 7 + CY, :] - op[field, x + 2, 9 : 9 + CY, :])
                )

            def dz(number):
                own = op[z_fields[number], x + 2, inner, :]
                edge = ez[number, x]
                below = jnp.where(lane >= CZ - 2, edge, own)
                above = jnp.where(lane < 2, edge, own)
                below_1 = jnp.where(lane >= CZ - 1, edge, own)
                above_1 = jnp.where(lane < 1, edge, own)
                return scale * (
                    (pltpu.roll(below, 2, 1) - pltpu.roll(above, CZ - 2, 1))
                    - 8.0 * (pltpu.roll(below_1, 1, 1) - pltpu.roll(above_1, CZ - 1, 1))
                )

            out[0, x] = -modulus * (dx(1) + dy(2) + dz(1))
            out[1, x] = -buoyancy * dx(0)
            out[2, x] = -buoyancy * dy(0)
            out[3, x] = -buoyancy * dz(0)
            out[4, x] = -(dx(5) + dy(6) + dz(3))
            out[5, x] = -dx(4)
            out[6, x] = -dy(4)
            out[7, x] = -dz(2)
            return carry

        lax.fori_loop(0, CX, step, 0)

    for load in loads[:3]:
        load.wait()
    operands(cs, cp, cc, cop)

    for number, field in enumerate(y_fields):
        ysend[0, number] = cop[field, 2 : 2 + CX, 8:10, :]
        ysend[1, number] = cop[field, 2 : 2 + CX, 6 + CY : 8 + CY, :]
    for block in range(2):
        packed = jnp.zeros((CY, CZ), jnp.float32)
        for j in range(32):
            number, x = divmod(block * 32 + j, CX)
            shifted = pltpu.roll(cop[z_fields[number], x + 2, inner, :], (4 * j + 2) % CZ, 1)
            packed = jnp.where((lane >= 4 * j) & (lane < 4 * j + 4), shifted, packed)
        zsend[block] = packed

    pl.semaphore_wait(barrier, expected)

    def halo_copies(axis, side):
        if axis == "gx":
            first = 2 if side == 0 else CX
            land = 2 + CX if side == 0 else 0
            return [
                pltpu.make_async_remote_copy(
                    src_ref=cop.at[pl.ds(start, 2), pl.ds(first, 2), pl.ds(8, CY)],
                    dst_ref=cop.at[pl.ds(start, 2), pl.ds(land, 2), pl.ds(8, CY)],
                    send_sem=hx_send.at[side, half],
                    recv_sem=hx_recv.at[1 - side, half],
                    device_id=neighbour(axis, side),
                    device_id_type=MESH,
                )
                for half, start in enumerate((0, 4))
            ]
        if axis == "gy":
            return [
                pltpu.make_async_remote_copy(
                    src_ref=ysend.at[side],
                    dst_ref=yhalo.at[1 - side],
                    send_sem=hy_send.at[side],
                    recv_sem=hy_recv.at[1 - side],
                    device_id=neighbour(axis, side),
                    device_id_type=MESH,
                )
            ]
        return [
            pltpu.make_async_remote_copy(
                src_ref=zsend,
                dst_ref=zhalo.at[1 - side],
                send_sem=hz_send.at[side],
                recv_sem=hz_recv.at[1 - side],
                device_id=neighbour(axis, side),
                device_id_type=MESH,
            )
        ]

    halos = {key: halo_copies(*key) for key in has}
    for key in has:

        @pl.when(has[key])
        def _():
            for copy in halos[key]:
                copy.start()

    for side in range(2):

        @pl.when(jnp.logical_not(has["gx", side]))
        def _():
            land = 0 if side == 0 else 2 + CX
            for field in x_fields:
                cop[field, land : land + 2, inner, :] = jnp.zeros((2, CY, CZ), jnp.float32)

        @pl.when(jnp.logical_not(has["gy", side]))
        def _():
            yhalo[side] = jnp.zeros(yhalo.shape[1:], jnp.float32)

        @pl.when(jnp.logical_not(has["gz", side]))
        def _():
            zhalo[side] = jnp.zeros(zhalo.shape[1:], jnp.float32)

    for load in loads[3:]:
        load.wait()
    operands(fs, fp, fc, fop)

    for key in has:

        @pl.when(has[key])
        def _():
            for copy in halos[key[0], 1 - key[1]]:
                copy.wait_recv()

    for number, field in enumerate(y_fields):
        cop[field, 2 : 2 + CX, 6:8, :] = yhalo[0, number]
        cop[field, 2 : 2 + CX, 8 + CY : 10 + CY, :] = yhalo[1, number]
    for block in range(2):
        merged = jnp.where((lane & 3) < 2, zhalo[0, block], zhalo[1, block])
        for j in range(32):
            number, x = divmod(block * 32 + j, CX)
            cez[number, x] = pltpu.roll(merged, (CZ - 4 * j - 2) % CZ, 1)

    for base, fields in ((0, x_fields), (32, y_fields)):
        for pair in range(2):
            for side in range(2):
                row = base + (pair * 2 + side) * 8
                values = []
                for field in fields[2 * pair : 2 * pair + 2]:
                    for candidate in range(2):
                        if base == 0:
                            at = 2 + candidate * PX + (PX if side else -1)
                            y0 = 8 + candidate * PY
                            values.append(cop[field, at, y0 : y0 + PY, :])
                        else:
                            at = 8 + candidate * PY + (PY if side else -1)
                            x0 = 2 + candidate * PX
                            values.append(cop[field, x0 : x0 + PX, at, :])
                left = lane_half < PZ
                rim_pair[0, row : row + 8, :] = jnp.where(
                    left, values[0], pltpu.roll(values[2], PZ, 1)
                )
                rim_pair[1, row : row + 8, :] = jnp.where(
                    left, pltpu.roll(values[1], PZ, 1), values[3]
                )
    for candidate in range(2):
        packed = jnp.zeros((PY, CZ), jnp.float32)
        y0 = candidate * PY
        for number, field in enumerate(z_fields):
            for x in range(PX):
                i = number * PX + x
                own = cop[field, 2 + candidate * PX + x, 8 + y0 : 8 + y0 + PY, :]
                edge = cez[number, candidate * PX + x, y0 : y0 + PY, :]
                if candidate == 0:
                    lower = pltpu.roll(edge, (4 * i - (CZ - 1)) % CZ, 1)
                    upper = pltpu.roll(own, (4 * i + 2 - PZ) % CZ, 1)
                else:
                    lower = pltpu.roll(own, (4 * i - (PZ - 1)) % CZ, 1)
                    upper = pltpu.roll(edge, (4 * i + 2) % CZ, 1)
                packed = jnp.where(
                    lane_half == 4 * i, lower, jnp.where(lane_half == 4 * i + 2, upper, packed)
                )
        rim_pair[candidate, 64:72, :] = packed + pltpu.roll(packed, 1, 1)

    second = dest_ref[1]
    rims = []
    for offset in range(1, count_x):
        rim_send[offset] = jnp.where(second == peers[offset], rim_pair[1], rim_pair[0])
        rims.append(
            pltpu.make_async_remote_copy(
                src_ref=rim_send.at[offset],
                dst_ref=rim_recv.at[offset],
                send_sem=rim_ss.at[offset],
                recv_sem=rim_rs.at[offset],
                device_id={"gx": peers[offset]},
                device_id_type=MESH,
            )
        )
        rims[-1].start()
    rim_recv[0] = jnp.where(second == me, rim_pair[1], rim_pair[0])

    slopes(cop, cez, cc, co, 1.0 / 12.0)

    for rim in rims:
        rim.wait_recv()
    parent = parent_ref[0]
    rim_now = rim_recv[lax.rem(me - parent + count_x, count_x)]
    row_number = lax.broadcasted_iota(jnp.int32, (CZ, CZ), 0)
    column_number = lax.broadcasted_iota(jnp.int32, (CZ, CZ), 1)
    spread = [
        (row_number == (column_number >> 1) + half * PZ).astype(jnp.bfloat16) for half in range(2)
    ]
    gather = [
        jnp.where((row_number >> 1) + half * PZ == column_number, 0.125, 0.0).astype(jnp.bfloat16)
        for half in range(2)
    ]
    for half in range(2):
        wide = split_dot(rim_now[:64], spread[half])
        xup[half, 0, pl.ds(0, 64, 2), :] = wide
        xup[half, 0, pl.ds(1, 64, 2), :] = wide
    zup[pl.ds(0, PY, 2), :] = rim_now[64:72]
    zup[pl.ds(1, PY, 2), :] = rim_now[64:72]
    for pair in range(2):
        for half in range(2):
            for side in range(2):
                row = (pair * 2 + side) * 16
                face = xup[half, 0, row : row + 16, :]
                land = 2 + CX if side else 0
                fop[x_fields[2 * pair + half], land, inner, :] = face
                fop[x_fields[2 * pair + half], land + 1, inner, :] = face
                land = 8 + CY if side else 6
                for x in range(CX):
                    at = 64 + row + x
                    fop[y_fields[2 * pair + half], 2 + x, land : land + 2, :] = jnp.broadcast_to(
                        xup[half, 0, at : at + 1, :], (2, CZ)
                    )
    spread_z = zup[...]
    for number in range(4):
        for x in range(PX):
            i = number * PX + x
            edge = pltpu.roll(spread_z, (CZ - 4 * i - 2) % CZ, 1)
            fez[number, 2 * x] = edge
            fez[number, 2 * x + 1] = edge

    slopes(fop, fez, fc, fo, 1.0 / 6.0)
    fine_out = pltpu.make_async_copy(fo, fo_hbm, out_sem.at[0])
    fine_out.start()

    sums = []
    for field in range(8):
        folded = fo[field].reshape(PX, 2, CY, CZ)
        pairs[field] = (folded[:, 0] + folded[:, 1]).reshape(PX * CY, CZ)
        sums.append(
            pairs[field, pl.ds(0, PX * PY, 2), :] + pairs[field, pl.ds(1, PX * PY, 2), :]
        )
    for field in range(4):
        avg[0, field] = split_dot(sums[field], gather[0]) + split_dot(sums[field + 4], gather[1])
    sends = []
    for offset in range(1, count_x):
        sends.append(
            pltpu.make_async_remote_copy(
                src_ref=avg.at[0],
                dst_ref=avg.at[offset],
                send_sem=avg_ss.at[offset],
                recv_sem=avg_rs.at[offset],
                device_id={"gx": peers[offset]},
                device_id_type=MESH,
            )
        )
        sends[-1].start()

    for send in sends:
        send.wait_recv()

    lane_box = lax.broadcasted_iota(jnp.int32, (PX, PY, CZ), 2)
    for candidate in range(2):
        target = dest_ref[candidate]
        slot = lax.rem(me - jnp.maximum(target, 0) + count_x, count_x)
        here = (lane_box < PZ) if candidate == 0 else (lane_box >= PZ)
        keep = here & (jnp.full((PX, PY, CZ), target, jnp.int32) >= 0)
        xs = slice(candidate * PX, candidate * PX + PX)
        ys = slice(candidate * PY, candidate * PY + PY)
        for field in range(4):
            got = avg[slot, field]
            turned = pltpu.roll(got, PZ, 1)
            low, high = (got, turned) if candidate == 0 else (turned, got)
            for number, value in ((field, low), (field + 4, high)):
                co[number, xs, ys, :] = jnp.where(
                    keep, value.reshape(PX, PY, CZ), co[number, xs, ys, :]
                )
    coarse_out = pltpu.make_async_copy(co, co_hbm, out_sem.at[1])
    coarse_out.start()

    for key in has:

        @pl.when(has[key])
        def _():
            for copy in halos[key]:
                copy.wait_send()

    for copy in rims + sends:
        copy.wait_send()
    fine_out.wait()
    coarse_out.wait()


def on_device(counts, cs, cp, cc, fs, fp, fc, fine_parent, patch_dest):
    shape = cs.shape
    CX, CY, CZ = shape[1:]
    PX, PY = CX // 2, CY // 2
    count_x = counts[0]
    anywhere = pl.BlockSpec(memory_space=pl.ANY)
    scalar = pl.BlockSpec(memory_space=pltpu.SMEM)
    vmem = lambda *dims: pltpu.VMEM(dims, jnp.float32)
    dma = pltpu.SemaphoreType.DMA
    coarse, fine = pl.pallas_call(
        functools.partial(kernel, counts),
        out_shape=(
            jax.ShapeDtypeStruct(shape, jnp.float32),
            jax.ShapeDtypeStruct(shape, jnp.float32),
        ),
        in_specs=[scalar, scalar] + [anywhere] * 6,
        out_specs=(anywhere, anywhere),
        scratch_shapes=[
            vmem(*shape),
            vmem(*shape),
            vmem(*cc.shape),
            vmem(*shape),
            vmem(*shape),
            vmem(*cc.shape),
            vmem(8, CX + 4, CY + 16, CZ),
            vmem(8, CX + 4, CY + 16, CZ),
            vmem(4, CX, CY, CZ),
            vmem(4, CX, CY, CZ),
            vmem(*shape),
            vmem(*shape),
            vmem(2, 4, CX, 2, CZ),
            vmem(2, 4, CX, 2, CZ),
            vmem(2, CY, CZ),
            vmem(2, 2, CY, CZ),
            vmem(2, 72, CZ),
            vmem(count_x, 72, CZ),
            vmem(count_x, 72, CZ),
            vmem(CY, CZ),
            vmem(2, 1, 128, CZ),
            vmem(8, PX * CY, CZ),
            vmem(count_x, 4, PX * PY, CZ),
            dma((6,)),
            dma((2,)),
            dma((2, 2)),
            dma((2, 2)),
            dma((2,)),
            dma((2,)),
            dma((2,)),
            dma((2,)),
            dma((count_x,)),
            dma((count_x,)),
            dma((count_x,)),
            dma((count_x,)),
        ],
        compiler_params=pltpu.CompilerParams(
            collective_id=0, has_side_effects=True, vmem_limit_bytes=40 * 1024 * 1024
        ),
        cost_estimate=pl.CostEstimate(flops=8_000_000, bytes_accessed=6_800_000, transcendentals=0),
    )(fine_parent.reshape(2), patch_dest.reshape(2), cs, cp, cc, fs, fp, fc)
    return coarse, fine


def solution(mesh):
    counts = tuple(mesh.shape[axis] for axis in ("gx", "gy", "gz"))
    field_spec = P(None, ("groups", "gx"), "gy", "gz")
    coefficient_spec = P(None, "gx", "gy", "gz")
    index_spec = P("gx", "gy", "gz", None)
    return jax.shard_map(
        functools.partial(on_device, counts),
        mesh=mesh,
        in_specs=(
            field_spec,
            field_spec,
            coefficient_spec,
            field_spec,
            field_spec,
            coefficient_spec,
            index_spec,
            index_spec,
        ),
        out_specs=(field_spec, field_spec),
        check_vma=False,
    )
```

```python
import functools

import jax
import jax.numpy as jnp
from jax import lax
from jax.experimental import pallas as pl
from jax.experimental.pallas import tpu as pltpu
from jax.sharding import PartitionSpec as P

section_weight = 0.1
MESH = pl.DeviceIdType.MESH
x_fields = (0, 1, 4, 5)
y_fields = (0, 2, 4, 6)
z_fields = (0, 3, 4, 7)


def split_dot(values, matrix):
    high = values.astype(jnp.bfloat16)
    low = (values - high.astype(jnp.float32)).astype(jnp.bfloat16)
    return jnp.dot(high, matrix, preferred_element_type=jnp.float32) + jnp.dot(
        low, matrix, preferred_element_type=jnp.float32
    )


def kernel(
    counts,
    parent_ref,
    dest_ref,
    cs_hbm,
    cp_hbm,
    cc_hbm,
    fs_hbm,
    fp_hbm,
    fc_hbm,
    co_hbm,
    fo_hbm,
    cs,
    cp,
    cc,
    fs,
    fp,
    fc,
    cop,
    fop,
    cez,
    fez,
    co,
    fo,
    ysend,
    yhalo,
    zsend,
    zhalo,
    rim_pair,
    rim_send,
    rim_recv,
    zup,
    xup,
    pairs,
    avg,
    edges,
    in_sem,
    out_sem,
    hx_send,
    hx_recv,
    hy_send,
    hy_recv,
    hz_send,
    hz_recv,
    rim_ss,
    rim_rs,
    avg_ss,
    avg_rs,
):
    count_x, count_y, count_z = counts
    CX, CY, CZ = cs.shape[1:]
    PX, PY, PZ = CX // 2, CY // 2, CZ // 2
    me = lax.axis_index("gx")
    my = lax.axis_index("gy")
    mz = lax.axis_index("gz")
    loads = [
        pltpu.make_async_copy(source, target, in_sem.at[number])
        for number, (source, target) in enumerate(
            ((cs_hbm, cs), (cp_hbm, cp), (cc_hbm, cc), (fs_hbm, fs), (fp_hbm, fp), (fc_hbm, fc))
        )
    ]
    for load in loads:
        load.start()

    peers = [lax.rem(me + offset, count_x) for offset in range(count_x)]
    barrier = pltpu.get_barrier_semaphore()
    for offset in range(1, count_x):
        pl.semaphore_signal(barrier, inc=1, device_id={"gx": peers[offset]}, device_id_type=MESH)
    has = {
        ("gx", 0): me > 0,
        ("gx", 1): me < count_x - 1,
        ("gy", 0): my > 0,
        ("gy", 1): my < count_y - 1,
        ("gz", 0): mz > 0,
        ("gz", 1): mz < count_z - 1,
    }
    index = {"gx": me, "gy": my, "gz": mz}
    count = {"gx": count_x, "gy": count_y, "gz": count_z}

    def neighbour(axis, side):
        return {axis: lax.rem(index[axis] + (1 if side else count[axis] - 1), count[axis])}

    for axis in ("gy", "gz"):
        for side in range(2):

            @pl.when(has[axis, side])
            def _():
                pl.semaphore_signal(
                    barrier, inc=1, device_id=neighbour(axis, side), device_id_type=MESH
                )

    expected = count_x - 1
    for axis in ("gy", "gz"):
        for side in range(2):
            expected = expected + has[axis, side].astype(jnp.int32)

    lane = lax.broadcasted_iota(jnp.int32, (CY, CZ), 1)
    lane_half = lax.broadcasted_iota(jnp.int32, (PY, CZ), 1)
    inner = slice(8, 8 + CY)

    def operands(state, previous, coefficient, target):
        def step(x, carry):
            modulus = coefficient[0, x]
            buoyancy = coefficient[1, x]
            for field in range(8):
                value = state[field, x] + section_weight * previous[field, x]
                if field == 4:
                    value = modulus * value
                if field > 4:
                    value = buoyancy * value
                target[field, x + 2, inner, :] = value
            return carry

        lax.fori_loop(0, CX, step, 0)

    def slopes(op, ez, coefficient, out, scale):
        def step(x, carry):
            modulus = coefficient[0, x]
            buoyancy = coefficient[1, x]

            def dx(field):
                return scale * (
                    (op[field, x, inner, :] - op[field, x + 4, inner, :])
                    - 8.0 * (op[field, x + 1, inner, :] - op[field, x + 3, inner, :])
                )

            def dy(field):
                return scale * (
                    (op[field, x + 2, 6 : 6 + CY, :] - op[field, x + 2, 10 : 10 + CY, :])
                    - 8.0 * (op[field, x + 2, 7 : 7 + CY, :] - op[field, x + 2, 9 : 9 + CY, :])
                )

            def dz(number):
                own = op[z_fields[number], x + 2, inner, :]
                edge = ez[number, x]
                below = jnp.where(lane >= CZ - 2, edge, own)
                above = jnp.where(lane < 2, edge, own)
                below_1 = jnp.where(lane >= CZ - 1, edge, own)
                above_1 = jnp.where(lane < 1, edge, own)
                return scale * (
                    (pltpu.roll(below, 2, 1) - pltpu.roll(above, CZ - 2, 1))
                    - 8.0 * (pltpu.roll(below_1, 1, 1) - pltpu.roll(above_1, CZ - 1, 1))
                )

            out[0, x] = -modulus * (dx(1) + dy(2) + dz(1))
            out[1, x] = -buoyancy * dx(0)
            out[2, x] = -buoyancy * dy(0)
            out[3, x] = -buoyancy * dz(0)
            out[4, x] = -(dx(5) + dy(6) + dz(3))
            out[5, x] = -dx(4)
            out[6, x] = -dy(4)
            out[7, x] = -dz(2)
            return carry

        lax.fori_loop(0, CX, step, 0)

    for load in loads[:3]:
        load.wait()
    operands(cs, cp, cc, cop)

    for number, field in enumerate(y_fields):
        ysend[0, number] = cop[field, 2 : 2 + CX, 8:10, :]
        ysend[1, number] = cop[field, 2 : 2 + CX, 6 + CY : 8 + CY, :]
    for block in range(2):
        packed = jnp.zeros((CY, CZ), jnp.float32)
        for j in range(32):
            number, x = divmod(block * 32 + j, CX)
            shifted = pltpu.roll(cop[z_fields[number], x + 2, inner, :], (4 * j + 2) % CZ, 1)
            packed = jnp.where((lane >= 4 * j) & (lane < 4 * j + 4), shifted, packed)
        zsend[block] = packed

    pl.semaphore_wait(barrier, expected)

    def halo_copies(axis, side):
        if axis == "gx":
            first = 2 if side == 0 else CX
            land = 2 + CX if side == 0 else 0
            return [
                pltpu.make_async_remote_copy(
                    src_ref=cop.at[pl.ds(start, 2), pl.ds(first, 2), pl.ds(8, CY)],
                    dst_ref=cop.at[pl.ds(start, 2), pl.ds(land, 2), pl.ds(8, CY)],
                    send_sem=hx_send.at[side, half],
                    recv_sem=hx_recv.at[1 - side, half],
                    device_id=neighbour(axis, side),
                    device_id_type=MESH,
                )
                for half, start in enumerate((0, 4))
            ]
        if axis == "gy":
            return [
                pltpu.make_async_remote_copy(
                    src_ref=ysend.at[side],
                    dst_ref=yhalo.at[1 - side],
                    send_sem=hy_send.at[side],
                    recv_sem=hy_recv.at[1 - side],
                    device_id=neighbour(axis, side),
                    device_id_type=MESH,
                )
            ]
        return [
            pltpu.make_async_remote_copy(
                src_ref=zsend,
                dst_ref=zhalo.at[1 - side],
                send_sem=hz_send.at[side],
                recv_sem=hz_recv.at[1 - side],
                device_id=neighbour(axis, side),
                device_id_type=MESH,
            )
        ]

    halos = {key: halo_copies(*key) for key in has}
    for key in has:

        @pl.when(has[key])
        def _():
            for copy in halos[key]:
                copy.start()

    for side in range(2):

        @pl.when(jnp.logical_not(has["gx", side]))
        def _():
            land = 0 if side == 0 else 2 + CX
            for field in x_fields:
                cop[field, land : land + 2, inner, :] = jnp.zeros((2, CY, CZ), jnp.float32)

        @pl.when(jnp.logical_not(has["gy", side]))
        def _():
            yhalo[side] = jnp.zeros(yhalo.shape[1:], jnp.float32)

        @pl.when(jnp.logical_not(has["gz", side]))
        def _():
            zhalo[side] = jnp.zeros(zhalo.shape[1:], jnp.float32)

    for load in loads[3:]:
        load.wait()
    operands(fs, fp, fc, fop)

    for field in range(8):
        for land in (0, 2 + CX):
            fop[field, land : land + 2, inner, :] = jnp.zeros((2, CY, CZ), jnp.float32)
    for field in y_fields:
        for land in (6, 8 + CY):
            fop[field, 2 : 2 + CX, land : land + 2, :] = jnp.zeros((CX, 2, CZ), jnp.float32)
    fez[...] = jnp.zeros(fez.shape, jnp.float32)
    slopes(fop, fez, fc, fo, 1.0 / 6.0)
    row_number = lax.broadcasted_iota(jnp.int32, (CZ, CZ), 0)
    column_number = lax.broadcasted_iota(jnp.int32, (CZ, CZ), 1)
    spread = [
        (row_number == (column_number >> 1) + half * PZ).astype(jnp.bfloat16) for half in range(2)
    ]
    gather = [
        jnp.where((row_number >> 1) + half * PZ == column_number, 0.125, 0.0).astype(jnp.bfloat16)
        for half in range(2)
    ]

    def quad_sums(number, values):
        folded = values.reshape(PX, 2, CY, CZ)
        pairs[number] = (folded[:, 0] + folded[:, 1]).reshape(PX * CY, CZ)
        return pairs[number, pl.ds(0, PX * PY, 2), :] + pairs[number, pl.ds(1, PX * PY, 2), :]

    sums = [quad_sums(field, fo[field]) for field in range(8)]
    for field in range(4):
        avg[0, field * 64 : field * 64 + 64, :] = split_dot(sums[field], gather[0]) + split_dot(
            sums[field + 4], gather[1]
        )
    sixth = 1.0 / 6.0
    edge_rows = []
    for half, number in enumerate((1, 0)):
        edges[half, 0:16, :] = sixth * (7.0 * fc[number, 0] - fc[number, 1])
        edges[half, 16:32, :] = sixth * (fc[number, CX - 2] - 7.0 * fc[number, CX - 1])
        edges[half, 32:48, :] = sixth * (7.0 * fc[number, :, 0, :] - fc[number, :, 1, :])
        edges[half, 48:64, :] = sixth * (
            fc[number, :, CY - 2, :] - 7.0 * fc[number, :, CY - 1, :]
        )
        edge_rows.append(
            edges[half, pl.ds(0, 32, 2), :] + edges[half, pl.ds(1, 32, 2), :]
        )
    avg[0, 256:288, :] = split_dot(edge_rows[0], gather[0]) + split_dot(edge_rows[1], gather[1])
    packed = jnp.where(
        lane_half < 64, 0.0, jnp.where((lane_half & 3) == 0, 0.5, -0.5)
    ) + jnp.zeros((PY, CZ), jnp.float32)
    for half, number in enumerate((1, 0)):
        whole = quad_sums(half, fc[number])
        for x in range(PX):
            i = half * PX + x
            block = whole[x * PY : x * PY + PY]
            lower = (0.125 * sixth) * (7.0 * block - pltpu.roll(block, CZ - 1, 1))
            upper = (0.125 * sixth) * (pltpu.roll(block, 1, 1) - 7.0 * block)
            packed = jnp.where(
                lane_half == 4 * i,
                pltpu.roll(lower, 4 * i, 1),
                jnp.where(
                    lane_half == 4 * i + 2,
                    pltpu.roll(upper, (4 * i + 2 - (CZ - 1)) % CZ, 1),
                    packed,
                ),
            )
    avg[0, 288:296, :] = packed

    sends = [
        [
            pltpu.make_async_remote_copy(
                src_ref=avg.at[0, pl.ds(start, size)],
                dst_ref=avg.at[offset, pl.ds(start, size)],
                send_sem=avg_ss.at[offset, part],
                recv_sem=avg_rs.at[offset, part],
                device_id={"gx": peers[offset]},
                device_id_type=MESH,
            )
            for offset in range(1, count_x)
        ]
        for part, (start, size) in enumerate(((0, 128), (128, 168)))
    ]
    for send in sends[0]:
        send.start()

    for key in has:

        @pl.when(has[key])
        def _():
            for copy in halos[key[0], 1 - key[1]]:
                copy.wait_recv()

    for number, field in enumerate(y_fields):
        cop[field, 2 : 2 + CX, 6:8, :] = yhalo[0, number]
        cop[field, 2 : 2 + CX, 8 + CY : 10 + CY, :] = yhalo[1, number]
    for block in range(2):
        merged = jnp.where((lane & 3) < 2, zhalo[0, block], zhalo[1, block])
        for j in range(32):
            number, x = divmod(block * 32 + j, CX)
            cez[number, x] = pltpu.roll(merged, (CZ - 4 * j - 2) % CZ, 1)

    for base, fields in ((0, x_fields), (32, y_fields)):
        for pair in range(2):
            for side in range(2):
                row = base + (pair * 2 + side) * 8
                values = []
                for field in fields[2 * pair : 2 * pair + 2]:
                    for candidate in range(2):
                        if base == 0:
                            at = 2 + candidate * PX + (PX if side else -1)
                            y0 = 8 + candidate * PY
                            values.append(cop[field, at, y0 : y0 + PY, :])
                        else:
                            at = 8 + candidate * PY + (PY if side else -1)
                            x0 = 2 + candidate * PX
                            values.append(cop[field, x0 : x0 + PX, at, :])
                left = lane_half < PZ
                rim_pair[0, row : row + 8, :] = jnp.where(
                    left, values[0], pltpu.roll(values[2], PZ, 1)
                )
                rim_pair[1, row : row + 8, :] = jnp.where(
                    left, pltpu.roll(values[1], PZ, 1), values[3]
                )
    for candidate in range(2):
        packed = jnp.zeros((PY, CZ), jnp.float32)
        y0 = candidate * PY
        for number, field in enumerate(z_fields):
            for x in range(PX):
                i = number * PX + x
                own = cop[field, 2 + candidate * PX + x, 8 + y0 : 8 + y0 + PY, :]
                edge = cez[number, candidate * PX + x, y0 : y0 + PY, :]
                if candidate == 0:
                    lower = pltpu.roll(edge, (4 * i - (CZ - 1)) % CZ, 1)
                    upper = pltpu.roll(own, (4 * i + 2 - PZ) % CZ, 1)
                else:
                    lower = pltpu.roll(own, (4 * i - (PZ - 1)) % CZ, 1)
                    upper = pltpu.roll(edge, (4 * i + 2) % CZ, 1)
                packed = jnp.where(
                    lane_half == 4 * i, lower, jnp.where(lane_half == 4 * i + 2, upper, packed)
                )
        rim_pair[candidate, 64:72, :] = packed + pltpu.roll(packed, 1, 1)

    second = dest_ref[1]
    rims = []
    for offset in range(1, count_x):
        rim_send[offset] = jnp.where(second == peers[offset], rim_pair[1], rim_pair[0])
        rims.append(
            pltpu.make_async_remote_copy(
                src_ref=rim_send.at[offset],
                dst_ref=rim_recv.at[offset],
                send_sem=rim_ss.at[offset],
                recv_sem=rim_rs.at[offset],
                device_id={"gx": peers[offset]},
                device_id_type=MESH,
            )
        )
        rims[-1].start()
    rim_recv[0] = jnp.where(second == me, rim_pair[1], rim_pair[0])

    for send in sends[1]:
        send.start()

    slopes(cop, cez, cc, co, 1.0 / 12.0)

    for rim in rims:
        rim.wait_recv()
    parent = parent_ref[0]
    rim_now = rim_recv[lax.rem(me - parent + count_x, count_x)]
    for half in range(2):
        wide = split_dot(rim_now[:64], spread[half])
        xup[half, 0, pl.ds(0, 64, 2), :] = wide
        xup[half, 0, pl.ds(1, 64, 2), :] = wide
    zup[pl.ds(0, PY, 2), :] = rim_now[64:72]
    zup[pl.ds(1, PY, 2), :] = rim_now[64:72]
    for pair in range(2):
        for half in range(2):
            for side in range(2):
                row = (pair * 2 + side) * 16
                face = xup[half, 0, row : row + 16, :]
                land = 2 + CX if side else 0
                fop[x_fields[2 * pair + half], land, inner, :] = face
                fop[x_fields[2 * pair + half], land + 1, inner, :] = face
                land = 8 + CY if side else 6
                for x in range(CX):
                    at = 64 + row + x
                    fop[y_fields[2 * pair + half], 2 + x, land : land + 2, :] = jnp.broadcast_to(
                        xup[half, 0, at : at + 1, :], (2, CZ)
                    )
    spread_z = zup[...]
    for number in range(4):
        for x in range(PX):
            i = number * PX + x
            edge = pltpu.roll(spread_z, (CZ - 4 * i - 2) % CZ, 1)
            fez[number, 2 * x] = edge
            fez[number, 2 * x + 1] = edge

    slopes(fop, fez, fc, fo, 1.0 / 6.0)
    fine_out = pltpu.make_async_copy(fo, fo_hbm, out_sem.at[0])
    fine_out.start()

    for send in sends[0] + sends[1]:
        send.wait_recv()

    lane_box = lax.broadcasted_iota(jnp.int32, (PX, PY, CZ), 2)
    for candidate in range(2):
        target = dest_ref[candidate]
        slot = lax.rem(me - jnp.maximum(target, 0) + count_x, count_x)
        here = (lane_box < PZ) if candidate == 0 else (lane_box >= PZ)
        keep = here & (jnp.full((PX, PY, CZ), target, jnp.int32) >= 0)
        xs = slice(candidate * PX, candidate * PX + PX)
        ys = slice(candidate * PY, candidate * PY + PY)
        for field in range(4):
            got = avg[slot, field * 64 : field * 64 + 64, :]
            turned = pltpu.roll(got, PZ, 1)
            low, high = (got, turned) if candidate == 0 else (turned, got)
            for number, value in ((field, low), (field + 4, high)):
                co[number, xs, ys, :] = jnp.where(
                    keep, value.reshape(PX, PY, CZ), co[number, xs, ys, :]
                )
        weights = avg[slot, 256:296, :]
        rim = rim_pair[candidate]
        keep_face = keep[0]
        zero = jnp.zeros((PY, CZ), jnp.float32)

        def halves(row):
            turned = pltpu.roll(row, PZ, 1)
            return (row, turned) if candidate == 0 else (turned, row)

        for side in range(2):
            sign = -0.5 if side else 0.5
            for base, outs in ((0, (1, 0, 5, 4)), (32, (2, 0, 6, 4))):
                row = base + side * 8
                scaled = weights[base // 2 + side * 8 : base // 2 + side * 8 + 8] * rim[
                    row : row + 8
                ]
                plain = sign * rim[row + 16 : row + 24]
                for number, value in zip(outs, halves(scaled) + halves(plain)):
                    value = jnp.where(keep_face, value, zero)
                    if base == 0:
                        at = candidate * PX + side * (PX - 1)
                        co[number, at, ys, :] += value
                    else:
                        at = candidate * PY + side * (PY - 1)
                        co[number, xs, at, :] += value
        shares = weights[32:40] * rim[64:72]
        first = candidate * PZ
        last = first + PZ - 1
        for order, number in enumerate((3, 0, 7, 4)):
            for x in range(PX):
                i = order * PX + x
                value = jnp.where(
                    lane_half == first,
                    pltpu.roll(shares, (first - 4 * i) % CZ, 1),
                    jnp.where(
                        lane_half == last, pltpu.roll(shares, (last - 4 * i - 2) % CZ, 1), zero
                    ),
                )
                co[number, candidate * PX + x, ys, :] += jnp.where(keep_face, value, zero)
    coarse_out = pltpu.make_async_copy(co, co_hbm, out_sem.at[1])
    coarse_out.start()

    for key in has:

        @pl.when(has[key])
        def _():
            for copy in halos[key]:
                copy.wait_send()

    for copy in rims + sends[0] + sends[1]:
        copy.wait_send()
    fine_out.wait()
    coarse_out.wait()


def on_device(counts, cs, cp, cc, fs, fp, fc, fine_parent, patch_dest):
    shape = cs.shape
    CX, CY, CZ = shape[1:]
    PX, PY = CX // 2, CY // 2
    count_x = counts[0]
    anywhere = pl.BlockSpec(memory_space=pl.ANY)
    scalar = pl.BlockSpec(memory_space=pltpu.SMEM)
    vmem = lambda *dims: pltpu.VMEM(dims, jnp.float32)
    dma = pltpu.SemaphoreType.DMA
    coarse, fine = pl.pallas_call(
        functools.partial(kernel, counts),
        out_shape=(
            jax.ShapeDtypeStruct(shape, jnp.float32),
            jax.ShapeDtypeStruct(shape, jnp.float32),
        ),
        in_specs=[scalar, scalar] + [anywhere] * 6,
        out_specs=(anywhere, anywhere),
        scratch_shapes=[
            vmem(*shape),
            vmem(*shape),
            vmem(*cc.shape),
            vmem(*shape),
            vmem(*shape),
            vmem(*cc.shape),
            vmem(8, CX + 4, CY + 16, CZ),
            vmem(8, CX + 4, CY + 16, CZ),
            vmem(4, CX, CY, CZ),
            vmem(4, CX, CY, CZ),
            vmem(*shape),
            vmem(*shape),
            vmem(2, 4, CX, 2, CZ),
            vmem(2, 4, CX, 2, CZ),
            vmem(2, CY, CZ),
            vmem(2, 2, CY, CZ),
            vmem(2, 72, CZ),
            vmem(count_x, 72, CZ),
            vmem(count_x, 72, CZ),
            vmem(CY, CZ),
            vmem(2, 1, 128, CZ),
            vmem(8, PX * CY, CZ),
            vmem(count_x, 4 * PX * PY + 40, CZ),
            vmem(2, 64, CZ),
            dma((6,)),
            dma((2,)),
            dma((2, 2)),
            dma((2, 2)),
            dma((2,)),
            dma((2,)),
            dma((2,)),
            dma((2,)),
            dma((count_x,)),
            dma((count_x,)),
            dma((count_x, 2)),
            dma((count_x, 2)),
        ],
        compiler_params=pltpu.CompilerParams(
            collective_id=0, has_side_effects=True, vmem_limit_bytes=60 * 1024 * 1024
        ),
        cost_estimate=pl.CostEstimate(flops=8_000_000, bytes_accessed=6_800_000, transcendentals=0),
    )(fine_parent.reshape(2), patch_dest.reshape(2), cs, cp, cc, fs, fp, fc)
    return coarse, fine


def solution(mesh):
    counts = tuple(mesh.shape[axis] for axis in ("gx", "gy", "gz"))
    field_spec = P(None, ("groups", "gx"), "gy", "gz")
    coefficient_spec = P(None, "gx", "gy", "gz")
    index_spec = P("gx", "gy", "gz", None)
    return jax.shard_map(
        functools.partial(on_device, counts),
        mesh=mesh,
        in_specs=(
            field_spec,
            field_spec,
            coefficient_spec,
            field_spec,
            field_spec,
            coefficient_spec,
            index_spec,
            index_spec,
        ),
        out_specs=(field_spec, field_spec),
        check_vma=False,
    )
```

```python
import functools

import jax
import jax.numpy as jnp
from jax import lax
from jax.experimental import pallas as pl
from jax.experimental.pallas import tpu as pltpu
from jax.sharding import PartitionSpec as P

section_weight = 0.1
MESH = pl.DeviceIdType.MESH
x_fields = (0, 1, 4, 5)
y_fields = (0, 2, 4, 6)
z_fields = (0, 3, 4, 7)


def split_dot(values, matrix):
    high = values.astype(jnp.bfloat16)
    low = (values - high.astype(jnp.float32)).astype(jnp.bfloat16)
    return jnp.dot(high, matrix, preferred_element_type=jnp.float32) + jnp.dot(
        low, matrix, preferred_element_type=jnp.float32
    )


def kernel(
    counts,
    parent_ref,
    dest_ref,
    cs_hbm,
    cp_hbm,
    cc_hbm,
    fs_hbm,
    fp_hbm,
    fc_hbm,
    co_hbm,
    fo_hbm,
    cs,
    cp,
    cc,
    fs,
    fp,
    fc,
    cop,
    fop,
    cez,
    fez,
    co,
    fo,
    ysend,
    yhalo,
    zsend,
    zhalo,
    rim_pair,
    rim_send,
    rim_recv,
    zup,
    xup,
    pairs,
    avg,
    edges,
    in_sem,
    out_sem,
    hx_send,
    hx_recv,
    hy_send,
    hy_recv,
    hz_send,
    hz_recv,
    rim_ss,
    rim_rs,
    avg_ss,
    avg_rs,
):
    count_x, count_y, count_z = counts
    CX, CY, CZ = cs.shape[1:]
    PX, PY, PZ = CX // 2, CY // 2, CZ // 2
    me = lax.axis_index("gx")
    my = lax.axis_index("gy")
    mz = lax.axis_index("gz")
    loads = [
        pltpu.make_async_copy(source, target, in_sem.at[number])
        for number, (source, target) in enumerate(
            ((cs_hbm, cs), (cp_hbm, cp), (cc_hbm, cc), (fs_hbm, fs), (fp_hbm, fp), (fc_hbm, fc))
        )
    ]
    for load in loads:
        load.start()

    peers = [lax.rem(me + offset, count_x) for offset in range(count_x)]
    barrier = pltpu.get_barrier_semaphore()
    for offset in range(1, count_x):
        pl.semaphore_signal(barrier, inc=1, device_id={"gx": peers[offset]}, device_id_type=MESH)
    has = {
        ("gx", 0): me > 0,
        ("gx", 1): me < count_x - 1,
        ("gy", 0): my > 0,
        ("gy", 1): my < count_y - 1,
        ("gz", 0): mz > 0,
        ("gz", 1): mz < count_z - 1,
    }
    index = {"gx": me, "gy": my, "gz": mz}
    count = {"gx": count_x, "gy": count_y, "gz": count_z}

    def neighbour(axis, side):
        return {axis: lax.rem(index[axis] + (1 if side else count[axis] - 1), count[axis])}

    for axis in ("gy", "gz"):
        for side in range(2):

            @pl.when(has[axis, side])
            def _():
                pl.semaphore_signal(
                    barrier, inc=1, device_id=neighbour(axis, side), device_id_type=MESH
                )

    expected = count_x - 1
    for axis in ("gy", "gz"):
        for side in range(2):
            expected = expected + has[axis, side].astype(jnp.int32)

    lane = lax.broadcasted_iota(jnp.int32, (CY, CZ), 1)
    lane_half = lax.broadcasted_iota(jnp.int32, (PY, CZ), 1)
    inner = slice(8, 8 + CY)

    def operands(state, previous, coefficient, target):
        def step(x, carry):
            modulus = coefficient[0, x]
            buoyancy = coefficient[1, x]
            for field in range(8):
                value = state[field, x] + section_weight * previous[field, x]
                if field == 4:
                    value = modulus * value
                if field > 4:
                    value = buoyancy * value
                target[field, x + 2, inner, :] = value
            return carry

        lax.fori_loop(0, CX, step, 0, unroll=4)

    def slopes(op, ez, coefficient, out, scale):
        def step(x, carry):
            modulus = coefficient[0, x]
            buoyancy = coefficient[1, x]

            def dx(field):
                return scale * (
                    (op[field, x, inner, :] - op[field, x + 4, inner, :])
                    - 8.0 * (op[field, x + 1, inner, :] - op[field, x + 3, inner, :])
                )

            def dy(field):
                return scale * (
                    (op[field, x + 2, 6 : 6 + CY, :] - op[field, x + 2, 10 : 10 + CY, :])
                    - 8.0 * (op[field, x + 2, 7 : 7 + CY, :] - op[field, x + 2, 9 : 9 + CY, :])
                )

            def dz(number):
                own = op[z_fields[number], x + 2, inner, :]
                edge = ez[number, x]
                below = jnp.where(lane >= CZ - 2, edge, own)
                above = jnp.where(lane < 2, edge, own)
                below_1 = jnp.where(lane >= CZ - 1, edge, own)
                above_1 = jnp.where(lane < 1, edge, own)
                return scale * (
                    (pltpu.roll(below, 2, 1) - pltpu.roll(above, CZ - 2, 1))
                    - 8.0 * (pltpu.roll(below_1, 1, 1) - pltpu.roll(above_1, CZ - 1, 1))
                )

            out[0, x] = -modulus * (dx(1) + dy(2) + dz(1))
            out[1, x] = -buoyancy * dx(0)
            out[2, x] = -buoyancy * dy(0)
            out[3, x] = -buoyancy * dz(0)
            out[4, x] = -(dx(5) + dy(6) + dz(3))
            out[5, x] = -dx(4)
            out[6, x] = -dy(4)
            out[7, x] = -dz(2)
            return carry

        lax.fori_loop(0, CX, step, 0, unroll=4)

    for load in loads[:3]:
        load.wait()
    operands(cs, cp, cc, cop)

    for number, field in enumerate(y_fields):
        ysend[0, number] = cop[field, 2 : 2 + CX, 8:10, :]
        ysend[1, number] = cop[field, 2 : 2 + CX, 6 + CY : 8 + CY, :]
    for block in range(2):
        packed = jnp.zeros((CY, CZ), jnp.float32)
        for j in range(32):
            number, x = divmod(block * 32 + j, CX)
            shifted = pltpu.roll(cop[z_fields[number], x + 2, inner, :], (4 * j + 2) % CZ, 1)
            packed = jnp.where((lane >= 4 * j) & (lane < 4 * j + 4), shifted, packed)
        zsend[block] = packed

    pl.semaphore_wait(barrier, expected)

    def halo_copies(axis, side):
        if axis == "gx":
            first = 2 if side == 0 else CX
            land = 2 + CX if side == 0 else 0
            return [
                pltpu.make_async_remote_copy(
                    src_ref=cop.at[pl.ds(start, 2), pl.ds(first, 2), pl.ds(8, CY)],
                    dst_ref=cop.at[pl.ds(start, 2), pl.ds(land, 2), pl.ds(8, CY)],
                    send_sem=hx_send.at[side, half],
                    recv_sem=hx_recv.at[1 - side, half],
                    device_id=neighbour(axis, side),
                    device_id_type=MESH,
                )
                for half, start in enumerate((0, 4))
            ]
        if axis == "gy":
            return [
                pltpu.make_async_remote_copy(
                    src_ref=ysend.at[side],
                    dst_ref=yhalo.at[1 - side],
                    send_sem=hy_send.at[side],
                    recv_sem=hy_recv.at[1 - side],
                    device_id=neighbour(axis, side),
                    device_id_type=MESH,
                )
            ]
        return [
            pltpu.make_async_remote_copy(
                src_ref=zsend,
                dst_ref=zhalo.at[1 - side],
                send_sem=hz_send.at[side],
                recv_sem=hz_recv.at[1 - side],
                device_id=neighbour(axis, side),
                device_id_type=MESH,
            )
        ]

    halos = {key: halo_copies(*key) for key in has}
    for key in has:

        @pl.when(has[key])
        def _():
            for copy in halos[key]:
                copy.start()

    for side in range(2):

        @pl.when(jnp.logical_not(has["gx", side]))
        def _():
            land = 0 if side == 0 else 2 + CX
            for field in x_fields:
                cop[field, land : land + 2, inner, :] = jnp.zeros((2, CY, CZ), jnp.float32)

        @pl.when(jnp.logical_not(has["gy", side]))
        def _():
            yhalo[side] = jnp.zeros(yhalo.shape[1:], jnp.float32)

        @pl.when(jnp.logical_not(has["gz", side]))
        def _():
            zhalo[side] = jnp.zeros(zhalo.shape[1:], jnp.float32)

    for load in loads[3:]:
        load.wait()
    operands(fs, fp, fc, fop)

    for field in range(8):
        for land in (0, 2 + CX):
            fop[field, land : land + 2, inner, :] = jnp.zeros((2, CY, CZ), jnp.float32)
    for field in y_fields:
        for land in (6, 8 + CY):
            fop[field, 2 : 2 + CX, land : land + 2, :] = jnp.zeros((CX, 2, CZ), jnp.float32)
    fez[...] = jnp.zeros(fez.shape, jnp.float32)
    slopes(fop, fez, fc, fo, 1.0 / 6.0)
    row_number = lax.broadcasted_iota(jnp.int32, (CZ, CZ), 0)
    column_number = lax.broadcasted_iota(jnp.int32, (CZ, CZ), 1)
    spread = [
        (row_number == (column_number >> 1) + half * PZ).astype(jnp.bfloat16) for half in range(2)
    ]
    gather = [
        jnp.where((row_number >> 1) + half * PZ == column_number, 0.125, 0.0).astype(jnp.bfloat16)
        for half in range(2)
    ]

    def quad_sums(number, values):
        folded = values.reshape(PX, 2, CY, CZ)
        pairs[number] = (folded[:, 0] + folded[:, 1]).reshape(PX * CY, CZ)
        return pairs[number, pl.ds(0, PX * PY, 2), :] + pairs[number, pl.ds(1, PX * PY, 2), :]

    sums = [quad_sums(field, fo[field]) for field in range(8)]
    for field in range(4):
        avg[0, field * 64 : field * 64 + 64, :] = split_dot(sums[field], gather[0]) + split_dot(
            sums[field + 4], gather[1]
        )
    sixth = 1.0 / 6.0
    edge_rows = []
    for half, number in enumerate((1, 0)):
        edges[half, 0:16, :] = sixth * (7.0 * fc[number, 0] - fc[number, 1])
        edges[half, 16:32, :] = sixth * (fc[number, CX - 2] - 7.0 * fc[number, CX - 1])
        edges[half, 32:48, :] = sixth * (7.0 * fc[number, :, 0, :] - fc[number, :, 1, :])
        edges[half, 48:64, :] = sixth * (
            fc[number, :, CY - 2, :] - 7.0 * fc[number, :, CY - 1, :]
        )
        edge_rows.append(
            edges[half, pl.ds(0, 32, 2), :] + edges[half, pl.ds(1, 32, 2), :]
        )
    avg[0, 256:288, :] = split_dot(edge_rows[0], gather[0]) + split_dot(edge_rows[1], gather[1])
    packed = jnp.where(
        lane_half < 64, 0.0, jnp.where((lane_half & 3) == 0, 0.5, -0.5)
    ) + jnp.zeros((PY, CZ), jnp.float32)
    for half, number in enumerate((1, 0)):
        whole = quad_sums(half, fc[number])
        for x in range(PX):
            i = half * PX + x
            block = whole[x * PY : x * PY + PY]
            lower = (0.125 * sixth) * (7.0 * block - pltpu.roll(block, CZ - 1, 1))
            upper = (0.125 * sixth) * (pltpu.roll(block, 1, 1) - 7.0 * block)
            packed = jnp.where(
                lane_half == 4 * i,
                pltpu.roll(lower, 4 * i, 1),
                jnp.where(
                    lane_half == 4 * i + 2,
                    pltpu.roll(upper, (4 * i + 2 - (CZ - 1)) % CZ, 1),
                    packed,
                ),
            )
    avg[0, 288:296, :] = packed

    sends = [
        [
            pltpu.make_async_remote_copy(
                src_ref=avg.at[0, pl.ds(start, size)],
                dst_ref=avg.at[offset, pl.ds(start, size)],
                send_sem=avg_ss.at[offset, part],
                recv_sem=avg_rs.at[offset, part],
                device_id={"gx": peers[offset]},
                device_id_type=MESH,
            )
            for offset in range(1, count_x)
        ]
        for part, (start, size) in enumerate(((0, 128), (128, 168)))
    ]
    for send in sends[0]:
        send.start()

    for key in has:

        @pl.when(has[key])
        def _():
            for copy in halos[key[0], 1 - key[1]]:
                copy.wait_recv()

    for number, field in enumerate(y_fields):
        cop[field, 2 : 2 + CX, 6:8, :] = yhalo[0, number]
        cop[field, 2 : 2 + CX, 8 + CY : 10 + CY, :] = yhalo[1, number]
    for block in range(2):
        merged = jnp.where((lane & 3) < 2, zhalo[0, block], zhalo[1, block])
        for j in range(32):
            number, x = divmod(block * 32 + j, CX)
            cez[number, x] = pltpu.roll(merged, (CZ - 4 * j - 2) % CZ, 1)

    for base, fields in ((0, x_fields), (32, y_fields)):
        for pair in range(2):
            for side in range(2):
                row = base + (pair * 2 + side) * 8
                values = []
                for field in fields[2 * pair : 2 * pair + 2]:
                    for candidate in range(2):
                        if base == 0:
                            at = 2 + candidate * PX + (PX if side else -1)
                            y0 = 8 + candidate * PY
                            values.append(cop[field, at, y0 : y0 + PY, :])
                        else:
                            at = 8 + candidate * PY + (PY if side else -1)
                            x0 = 2 + candidate * PX
                            values.append(cop[field, x0 : x0 + PX, at, :])
                left = lane_half < PZ
                rim_pair[0, row : row + 8, :] = jnp.where(
                    left, values[0], pltpu.roll(values[2], PZ, 1)
                )
                rim_pair[1, row : row + 8, :] = jnp.where(
                    left, pltpu.roll(values[1], PZ, 1), values[3]
                )
    for candidate in range(2):
        packed = jnp.zeros((PY, CZ), jnp.float32)
        y0 = candidate * PY
        for number, field in enumerate(z_fields):
            for x in range(PX):
                i = number * PX + x
                own = cop[field, 2 + candidate * PX + x, 8 + y0 : 8 + y0 + PY, :]
                edge = cez[number, candidate * PX + x, y0 : y0 + PY, :]
                if candidate == 0:
                    lower = pltpu.roll(edge, (4 * i - (CZ - 1)) % CZ, 1)
                    upper = pltpu.roll(own, (4 * i + 2 - PZ) % CZ, 1)
                else:
                    lower = pltpu.roll(own, (4 * i - (PZ - 1)) % CZ, 1)
                    upper = pltpu.roll(edge, (4 * i + 2) % CZ, 1)
                packed = jnp.where(
                    lane_half == 4 * i, lower, jnp.where(lane_half == 4 * i + 2, upper, packed)
                )
        rim_pair[candidate, 64:72, :] = packed + pltpu.roll(packed, 1, 1)

    second = dest_ref[1]
    rims = []
    for offset in range(1, count_x):
        rim_send[offset] = jnp.where(second == peers[offset], rim_pair[1], rim_pair[0])
        rims.append(
            pltpu.make_async_remote_copy(
                src_ref=rim_send.at[offset],
                dst_ref=rim_recv.at[offset],
                send_sem=rim_ss.at[offset],
                recv_sem=rim_rs.at[offset],
                device_id={"gx": peers[offset]},
                device_id_type=MESH,
            )
        )
        rims[-1].start()
    rim_recv[0] = jnp.where(second == me, rim_pair[1], rim_pair[0])

    for send in sends[1]:
        send.start()

    slopes(cop, cez, cc, co, 1.0 / 12.0)

    for rim in rims:
        rim.wait_recv()
    parent = parent_ref[0]
    rim_now = rim_recv[lax.rem(me - parent + count_x, count_x)]
    for half in range(2):
        wide = split_dot(rim_now[:64], spread[half])
        xup[half, 0, pl.ds(0, 64, 2), :] = wide
        xup[half, 0, pl.ds(1, 64, 2), :] = wide
    zup[pl.ds(0, PY, 2), :] = rim_now[64:72]
    zup[pl.ds(1, PY, 2), :] = rim_now[64:72]
    for pair in range(2):
        for half in range(2):
            for side in range(2):
                row = (pair * 2 + side) * 16
                face = xup[half, 0, row : row + 16, :]
                land = 2 + CX if side else 0
                fop[x_fields[2 * pair + half], land, inner, :] = face
                fop[x_fields[2 * pair + half], land + 1, inner, :] = face
                land = 8 + CY if side else 6
                for x in range(CX):
                    at = 64 + row + x
                    fop[y_fields[2 * pair + half], 2 + x, land : land + 2, :] = jnp.broadcast_to(
                        xup[half, 0, at : at + 1, :], (2, CZ)
                    )
    spread_z = zup[...]
    for number in range(4):
        for x in range(PX):
            i = number * PX + x
            edge = pltpu.roll(spread_z, (CZ - 4 * i - 2) % CZ, 1)
            fez[number, 2 * x] = edge
            fez[number, 2 * x + 1] = edge

    slopes(fop, fez, fc, fo, 1.0 / 6.0)
    fine_out = pltpu.make_async_copy(fo, fo_hbm, out_sem.at[0])
    fine_out.start()

    for send in sends[0] + sends[1]:
        send.wait_recv()

    lane_box = lax.broadcasted_iota(jnp.int32, (PX, PY, CZ), 2)
    for candidate in range(2):
        target = dest_ref[candidate]
        slot = lax.rem(me - jnp.maximum(target, 0) + count_x, count_x)
        here = (lane_box < PZ) if candidate == 0 else (lane_box >= PZ)
        keep = here & (jnp.full((PX, PY, CZ), target, jnp.int32) >= 0)
        xs = slice(candidate * PX, candidate * PX + PX)
        ys = slice(candidate * PY, candidate * PY + PY)
        for field in range(4):
            got = avg[slot, field * 64 : field * 64 + 64, :]
            turned = pltpu.roll(got, PZ, 1)
            low, high = (got, turned) if candidate == 0 else (turned, got)
            for number, value in ((field, low), (field + 4, high)):
                co[number, xs, ys, :] = jnp.where(
                    keep, value.reshape(PX, PY, CZ), co[number, xs, ys, :]
                )
        weights = avg[slot, 256:296, :]
        rim = rim_pair[candidate]
        keep_face = keep[0]
        zero = jnp.zeros((PY, CZ), jnp.float32)

        def halves(row):
            turned = pltpu.roll(row, PZ, 1)
            return (row, turned) if candidate == 0 else (turned, row)

        for side in range(2):
            sign = -0.5 if side else 0.5
            for base, outs in ((0, (1, 0, 5, 4)), (32, (2, 0, 6, 4))):
                row = base + side * 8
                scaled = weights[base // 2 + side * 8 : base // 2 + side * 8 + 8] * rim[
                    row : row + 8
                ]
                plain = sign * rim[row + 16 : row + 24]
                for number, value in zip(outs, halves(scaled) + halves(plain)):
                    value = jnp.where(keep_face, value, zero)
                    if base == 0:
                        at = candidate * PX + side * (PX - 1)
                        co[number, at, ys, :] += value
                    else:
                        at = candidate * PY + side * (PY - 1)
                        co[number, xs, at, :] += value
        shares = weights[32:40] * rim[64:72]
        first = candidate * PZ
        last = first + PZ - 1
        for order, number in enumerate((3, 0, 7, 4)):
            for x in range(PX):
                i = order * PX + x
                value = jnp.where(
                    lane_half == first,
                    pltpu.roll(shares, (first - 4 * i) % CZ, 1),
                    jnp.where(
                        lane_half == last, pltpu.roll(shares, (last - 4 * i - 2) % CZ, 1), zero
                    ),
                )
                co[number, candidate * PX + x, ys, :] += jnp.where(keep_face, value, zero)
    coarse_out = pltpu.make_async_copy(co, co_hbm, out_sem.at[1])
    coarse_out.start()

    for key in has:

        @pl.when(has[key])
        def _():
            for copy in halos[key]:
                copy.wait_send()

    for copy in rims + sends[0] + sends[1]:
        copy.wait_send()
    fine_out.wait()
    coarse_out.wait()


def on_device(counts, cs, cp, cc, fs, fp, fc, fine_parent, patch_dest):
    shape = cs.shape
    CX, CY, CZ = shape[1:]
    PX, PY = CX // 2, CY // 2
    count_x = counts[0]
    anywhere = pl.BlockSpec(memory_space=pl.ANY)
    scalar = pl.BlockSpec(memory_space=pltpu.SMEM)
    vmem = lambda *dims: pltpu.VMEM(dims, jnp.float32)
    dma = pltpu.SemaphoreType.DMA
    coarse, fine = pl.pallas_call(
        functools.partial(kernel, counts),
        out_shape=(
            jax.ShapeDtypeStruct(shape, jnp.float32),
            jax.ShapeDtypeStruct(shape, jnp.float32),
        ),
        in_specs=[scalar, scalar] + [anywhere] * 6,
        out_specs=(anywhere, anywhere),
        scratch_shapes=[
            vmem(*shape),
            vmem(*shape),
            vmem(*cc.shape),
            vmem(*shape),
            vmem(*shape),
            vmem(*cc.shape),
            vmem(8, CX + 4, CY + 16, CZ),
            vmem(8, CX + 4, CY + 16, CZ),
            vmem(4, CX, CY, CZ),
            vmem(4, CX, CY, CZ),
            vmem(*shape),
            vmem(*shape),
            vmem(2, 4, CX, 2, CZ),
            vmem(2, 4, CX, 2, CZ),
            vmem(2, CY, CZ),
            vmem(2, 2, CY, CZ),
            vmem(2, 72, CZ),
            vmem(count_x, 72, CZ),
            vmem(count_x, 72, CZ),
            vmem(CY, CZ),
            vmem(2, 1, 128, CZ),
            vmem(8, PX * CY, CZ),
            vmem(count_x, 4 * PX * PY + 40, CZ),
            vmem(2, 64, CZ),
            dma((6,)),
            dma((2,)),
            dma((2, 2)),
            dma((2, 2)),
            dma((2,)),
            dma((2,)),
            dma((2,)),
            dma((2,)),
            dma((count_x,)),
            dma((count_x,)),
            dma((count_x, 2)),
            dma((count_x, 2)),
        ],
        compiler_params=pltpu.CompilerParams(
            collective_id=0, has_side_effects=True, vmem_limit_bytes=60 * 1024 * 1024
        ),
        cost_estimate=pl.CostEstimate(flops=8_000_000, bytes_accessed=6_800_000, transcendentals=0),
    )(fine_parent.reshape(2), patch_dest.reshape(2), cs, cp, cc, fs, fp, fc)
    return coarse, fine


def solution(mesh):
    counts = tuple(mesh.shape[axis] for axis in ("gx", "gy", "gz"))
    field_spec = P(None, ("groups", "gx"), "gy", "gz")
    coefficient_spec = P(None, "gx", "gy", "gz")
    index_spec = P("gx", "gy", "gz", None)
    return jax.shard_map(
        functools.partial(on_device, counts),
        mesh=mesh,
        in_specs=(
            field_spec,
            field_spec,
            coefficient_spec,
            field_spec,
            field_spec,
            coefficient_spec,
            index_spec,
            index_spec,
        ),
        out_specs=(field_spec, field_spec),
        check_vma=False,
    )
```
